768 devices in a mesh: table: 48 (over z, x), col: 16 (over y, core).
Axes of the slice: x: 4, y: 8, z: 12, core: 2. Of those that a mesh axis runs over, the one named last changes fastest.
Arguments:
- pooled_grad: bfloat16 [96, 512, 12288], P(None, 'col', 'table'), may hold values from -2.7 to 2.7
- row_ids: int32 [96, 4, 12288], P(None, None, 'table'), may hold values from 0 to 1023
- lengths: int32 [96, 12288], P(None, 'table'), may hold values from 1 to 4
- feature_order: int32 [96], replicated, may hold values from 0 to 95, each once
- weights: float32 [96, 512, 1024], P('table', 'col'), may hold values from -3 to 3
- state: float32 [96, 1024], P('table'), may hold values from 0.1 to 10
Outputs:
- new_weights: float32 [96, 512, 1024], P('table', 'col')
- new_state: float32 [96, 1024], P('table')
The draws below stay inside these ranges and needn't reach their ends.
All inputs are finite; a program needn't handle non-finite values.
Results may differ from the reference program's by a relative error of at most 0.0003.
Values may be sent and summed in bfloat16 or wider, within the bound.
A program may use at most 32 MiB of HBM per device.

```python
import math
import jax
import jax.numpy as jnp
import numpy as np
from jax import lax

FEATURES = 96
D = 512
POOL = 4
ROWS = 1024
SAMPLES = 12288


def draw_pooled_grad(key, part):
    key = jax.random.fold_in(key, 11)
    rising = jnp.arange(D, dtype=jnp.float32) / D
    values = jnp.clip(jax.random.normal(key, (FEATURES, D, SAMPLES), jnp.float32), -6.0, 6.0)
    factor = 3.0 ** rising
    return (0.15 * values * factor[None, :, None]).astype(jnp.bfloat16)


def plant(drawn, stream_key, least, top_value):
    longest = drawn.shape.index(max(drawn.shape))
    spots = []
    for shift in (0, 1):
        where = [jax.random.randint(jax.random.fold_in(stream_key, axis), (), 0, length) for axis, length in enumerate(drawn.shape)]
        where[longest] = (where[longest] + shift) % drawn.shape[longest]
        spots.append(tuple(where))
    return drawn.at[spots[0]].set(least).at[spots[1]].set(top_value)


def block_levels(key, extent, split, smallest, high):
    factor_of = 1.0
    for dim, parts in split:
        steps = jax.random.uniform(jax.random.fold_in(jax.random.fold_in(key, 6), dim), (parts,), jnp.float32, smallest / len(split), high / len(split))
        factor_of = factor_of * jnp.repeat(jnp.exp(steps), extent[dim] // parts).reshape((-1,) + (1,) * (len(extent) - 1 - dim))
    return factor_of


def cumulative_ranks(amount, slope):
    weights = [(1 << 20) // math.isqrt(grade ** slope) + 1 for grade in range(1, amount + 1)]
    spread = 1 + sum(weights) // (1 << 30)
    return np.cumsum(np.array([max(1, weight // spread) for weight in weights]))


def skewed_ids(stream_key, dims, amount, lean):
    grid = cumulative_ranks(amount, lean)
    pick = jax.random.randint(jax.random.fold_in(stream_key, 1), dims, 0, int(grid[amount - 1]))
    grade = jnp.searchsorted(jnp.asarray(grid, jnp.int32), pick, side="right")
    return jax.random.permutation(jax.random.fold_in(stream_key, 2), amount)[grade].astype(jnp.int32)


def scatter_about(stream_key, shape, deviation, bound, shards=(), kind=jnp.bfloat16):
    result = jax.random.normal(stream_key, shape, jnp.float32) * deviation
    if len(shards) > 0:
        result = block_levels(stream_key, shape, shards, -0.22, 0.18) * result
    return jnp.clip(result, min=-bound, max=bound).astype(kind)


def setup_inputs(seed: int = 0) -> dict:
    key_list = jax.random.split(jax.random.key(seed), 7)
    return {
        "pooled_grad": draw_pooled_grad(jax.random.fold_in(key_list[6], 71), 0),
        "row_ids": plant(skewed_ids(key_list[1], (FEATURES, POOL, SAMPLES), ROWS, 2), jax.random.fold_in(key_list[1], 3), 0, ROWS - 1).astype(jnp.int32),
        "lengths": plant(jax.random.randint(key_list[2], (FEATURES, SAMPLES), 1, POOL + 1), jax.random.fold_in(key_list[2], 1), 1, POOL).astype(jnp.int32),
        "feature_order": jax.random.permutation(key_list[3], FEATURES).astype(jnp.int32),
        "weights": scatter_about(key_list[4], (FEATURES, D, ROWS), 0.5, 3.0, ((0, 48), (1, 16)), jnp.float32),
        "state": jnp.clip(jnp.exp(math.log(10.0) - 4.6051702 * jax.random.uniform(key_list[5], (FEATURES, ROWS), jnp.float32) ** block_levels(key_list[5], (FEATURES, ROWS), ((0, 48),), -0.2, 0.2)), 0.1, 10.0),
    }


def reference(pooled_grad, row_ids, lengths, feature_order, weights, state):
    position = lax.broadcasted_iota(jnp.int32, row_ids.shape, 1)
    live_ids = jnp.where(position < lengths[:, None, :], row_ids, -1)
    live_ids = jnp.take(live_ids, feature_order, axis=0)
    ordered = jnp.take(pooled_grad, feature_order, axis=0)
    columns = jnp.arange(ROWS, dtype=jnp.int32)

    def one_slot(paired):
        slot_ids, slot_grad = paired
        counts = jnp.zeros((SAMPLES, ROWS), jnp.float32)
        for place in range(POOL):
            counts = counts + (slot_ids[place][:, None] == columns[None, :]).astype(jnp.float32)
        counts = counts.astype(jnp.bfloat16).astype(jnp.float32)
        return jnp.dot(slot_grad.astype(jnp.float32), counts, precision=lax.Precision.HIGHEST, preferred_element_type=jnp.float32)
    row_grad = lax.map(one_slot, (live_ids, ordered))
    new_state = state + lax.optimization_barrier(jnp.sum(row_grad * row_grad, axis=1)) / D
    new_weights = weights - 0.3 * row_grad / jnp.sqrt(new_state)[:, None, :]
    return (new_weights, new_state)
```

```python
import functools

import jax
import jax.numpy as jnp
from jax import lax
from jax.experimental import pallas as pl
from jax.experimental.pallas import tpu as pltpu
from jax.sharding import PartitionSpec as P

MESH = pl.DeviceIdType.MESH
LOW = 256


def kernel(
    tables, cols, width, place_count, order_ref, grad_ref, ids_ref, len_ref, w_ref, state_ref,
    new_w_ref, new_state_ref,
    send_grad, recv_grad, send_ids, all_ids, acc, squares,
    gs_sem, gr_sem, is_sem, ir_sem, cs_sem, cr_sem, qs_sem, qr_sem,
):
    t = lax.axis_index("table")
    c = lax.axis_index("col")
    slots = w_ref.shape[0]
    dim = w_ref.shape[1]
    rows = w_ref.shape[2]
    samples = grad_ref.shape[2]
    highs = rows // LOW
    across = 4 if tables % 4 == 0 else 1
    deep = tables // across
    shares = tables // cols

    def partner(step, sign):
        q = step // across
        dx = step % across
        far = (q + 1) // 2
        dz = (q % 2) * far + (1 - q % 2) * (deep - far)
        z = t // across
        x = t % across
        pz = (z + sign * dz + 2 * deep) % deep
        px = (x + sign * dx + 2 * across) % across
        return pz * across + px

    barrier = pltpu.get_barrier_semaphore()

    @pl.loop(1, tables)
    def _(step):
        pl.semaphore_signal(barrier, inc=1, device_id=(partner(step, 1), c), device_id_type=MESH)

    @pl.loop(1, cols)
    def _(step):
        pl.semaphore_signal(barrier, inc=1, device_id=(t, (c + step) % cols), device_id_type=MESH)

    place = lax.broadcasted_iota(jnp.int32, (place_count, samples), 0)

    def ids_target(share):
        return (c - t % cols + cols) % cols + cols * share

    for share in range(shares):
        target = ids_target(share)
        live = []
        for slot in range(slots):
            feature = order_ref[slots * target + slot]
            length = len_ref[pl.ds(feature, 1), :]
            live.append(jnp.where(place < length, ids_ref[feature], -1))
        send_ids[share] = jnp.concatenate(live, axis=0)

    acc[...] = jnp.zeros_like(acc)
    for slot in range(slots):
        recv_grad[t, slot] = grad_ref[order_ref[slots * t + slot]]

    pl.semaphore_wait(barrier, tables - 1 + cols - 1)

    def ids_copy(share):
        return pltpu.make_async_remote_copy(
            src_ref=send_ids.at[share],
            dst_ref=all_ids.at[c, t // cols],
            send_sem=is_sem.at[share],
            recv_sem=ir_sem.at[t // cols],
            device_id=(ids_target(share), c),
            device_id_type=MESH,
        )

    for share in range(shares):
        @pl.when(ids_target(share) == t)
        def _():
            all_ids[c, t // cols] = send_ids[share]

        @pl.when(ids_target(share) != t)
        def _():
            ids_copy(share).start()

    def grad_copy(target):
        return pltpu.make_async_remote_copy(
            src_ref=send_grad.at[target],
            dst_ref=recv_grad.at[t],
            send_sem=gs_sem.at[target],
            recv_sem=gr_sem.at[t],
            device_id=(target, c),
            device_id_type=MESH,
        )

    @pl.loop(1, tables)
    def _(step):
        target = partner(step, 1)
        for slot in range(slots):
            send_grad[target, slot] = grad_ref[order_ref[slots * target + slot]]
        grad_copy(target).start()

    def ids_arrival(share):
        return pltpu.make_async_remote_copy(
            src_ref=send_ids.at[share],
            dst_ref=all_ids.at[c, share],
            send_sem=is_sem.at[share],
            recv_sem=ir_sem.at[share],
            device_id=(ids_target(share), c),
            device_id_type=MESH,
        )

    for share in range(shares):
        @pl.when(ids_target(share) != t)
        def _():
            ids_arrival(share).wait_recv()

    def col_ids(peer):
        return pltpu.make_async_remote_copy(
            src_ref=all_ids.at[c],
            dst_ref=all_ids.at[c],
            send_sem=cs_sem.at[peer],
            recv_sem=cr_sem.at[c],
            device_id=(t, peer),
            device_id_type=MESH,
        )

    def col_ids_arrival(peer):
        return pltpu.make_async_remote_copy(
            src_ref=all_ids.at[peer],
            dst_ref=all_ids.at[peer],
            send_sem=cs_sem.at[peer],
            recv_sem=cr_sem.at[peer],
            device_id=(t, peer),
            device_id_type=MESH,
        )

    @pl.loop(1, cols)
    def _(step):
        col_ids((c + step) % cols).start()

    @pl.loop(1, cols)
    def _(step):
        col_ids_arrival((c - step + cols) % cols).wait_recv()

    low_line = lax.broadcasted_iota(jnp.int32, (LOW, samples), 0)
    zero = jnp.zeros((dim, samples), jnp.bfloat16)

    def work(source):
        block = all_ids[(source + t) % cols, source // cols]
        high = block >> 8
        low = block & (LOW - 1)
        for slot in range(slots):
            grad = recv_grad[source, slot]
            left, right = [], []
            for p in range(place_count):
                row = slot * place_count + p
                low_row = jnp.broadcast_to(low[row:row + 1], (LOW, samples))
                right.append(jnp.where(low_row == low_line, 1.0, 0.0).astype(jnp.bfloat16))
                high_row = jnp.broadcast_to(high[row:row + 1], (dim, samples))
                left.append(jnp.concatenate(
                    [grad * jnp.where(high_row == h, 1.0, 0.0).astype(jnp.bfloat16) for h in range(highs)], axis=0))
            acc[slot] += lax.dot_general(
                jnp.concatenate(left, axis=1), jnp.concatenate(right, axis=1),
                (((1,), (1,)), ((), ())), preferred_element_type=jnp.float32)

    work(t)

    @pl.loop(1, tables)
    def _(step):
        source = partner(step, -1)
        pltpu.make_async_remote_copy(
            src_ref=send_grad.at[source],
            dst_ref=recv_grad.at[source],
            send_sem=gs_sem.at[source],
            recv_sem=gr_sem.at[source],
            device_id=(source, c),
            device_id_type=MESH,
        ).wait_recv()
        work(source)

    sums = []
    for slot in range(slots):
        for h in range(highs):
            part = acc[slot, h * dim:(h + 1) * dim, :]
            sums.append(jnp.sum(part * part, axis=0, keepdims=True))
    squares[c] = jnp.concatenate(sums, axis=0)

    def square_copy(peer, owner):
        return pltpu.make_async_remote_copy(
            src_ref=squares.at[owner],
            dst_ref=squares.at[owner],
            send_sem=qs_sem.at[peer],
            recv_sem=qr_sem.at[owner],
            device_id=(t, peer),
            device_id_type=MESH,
        )

    @pl.loop(1, cols)
    def _(step):
        square_copy((c + step) % cols, c).start()

    @pl.loop(1, cols)
    def _(step):
        peer = (c - step + cols) % cols
        square_copy(peer, peer).wait_recv()

    total = squares[0]
    for peer in range(1, cols):
        total = total + squares[peer]
    full = dim * cols
    for slot in range(slots):
        for h in range(highs):
            row = slot * highs + h
            span = slice(h * LOW, (h + 1) * LOW)
            new_state = state_ref[slot:slot + 1, span] + total[row:row + 1] / full
            new_state_ref[slot:slot + 1, span] = new_state
            scale = 0.3 / jnp.sqrt(new_state)
            new_w_ref[slot, :, span] = w_ref[slot, :, span] - acc[slot, h * dim:(h + 1) * dim, :] * scale

    for share in range(shares):
        @pl.when(ids_target(share) != t)
        def _():
            ids_copy(share).wait_send()

    @pl.loop(1, cols)
    def _(step):
        peer = (c + step) % cols
        col_ids(peer).wait_send()
        square_copy(peer, c).wait_send()

    @pl.loop(1, tables)
    def _(step):
        grad_copy(partner(step, 1)).wait_send()


def solution(mesh):
    tables, cols = mesh.shape["table"], mesh.shape["col"]

    def body(pooled_grad, row_ids, lengths, feature_order, weights, state):
        features, width, samples = pooled_grad.shape
        place_count = row_ids.shape[1]
        slots, dim, rows = weights.shape
        shares = tables // cols
        vmem = pl.BlockSpec(memory_space=pltpu.VMEM)
        dma = pltpu.SemaphoreType.DMA
        return pl.pallas_call(
            functools.partial(kernel, tables, cols, width, place_count),
            out_shape=(
                jax.ShapeDtypeStruct(weights.shape, jnp.float32),
                jax.ShapeDtypeStruct(state.shape, jnp.float32),
            ),
            in_specs=[pl.BlockSpec(memory_space=pltpu.SMEM)] + [vmem] * 5,
            out_specs=(vmem, vmem),
            scratch_shapes=[
                pltpu.VMEM((tables, slots, dim, samples), jnp.bfloat16),
                pltpu.VMEM((tables, slots, dim, samples), jnp.bfloat16),
                pltpu.VMEM((shares, slots * place_count, samples), jnp.int32),
                pltpu.VMEM((cols, shares, slots * place_count, samples), jnp.int32),
                pltpu.VMEM((slots, rows // LOW * dim, LOW), jnp.float32),
                pltpu.VMEM((cols, slots * (rows // LOW), LOW), jnp.float32),
                dma((tables,)), dma((tables,)),
                dma((shares,)), dma((shares,)),
                dma((cols,)), dma((cols,)),
                dma((cols,)), dma((cols,)),
            ],
            compiler_params=pltpu.CompilerParams(
                collective_id=0, has_side_effects=True, vmem_limit_bytes=32 * 1024 * 1024
            ),
            cost_estimate=pl.CostEstimate(
                flops=4 * slots * tables * samples * rows * dim, bytes_accessed=4 * 1024 * 1024, transcendentals=0
            ),
        )(feature_order, pooled_grad, row_ids, lengths, weights, state)

    return jax.shard_map(
        body,
        mesh=mesh,
        in_specs=(
            P(None, "col", "table"),
            P(None, None, "table"),
            P(None, "table"),
            P(),
            P("table", "col", None),
            P("table", None),
        ),
        out_specs=(P("table", "col", None), P("table", None)),
        check_vma=False,
    )
```

```python
import functools

import jax
import jax.numpy as jnp
from jax import lax
from jax.experimental import pallas as pl
from jax.experimental.pallas import tpu as pltpu
from jax.sharding import PartitionSpec as P

MESH = pl.DeviceIdType.MESH
LOW = 256


def kernel(
    tables, cols, place_count, order_hbm, grad_hbm, ids_hbm, len_hbm, w_hbm, state_hbm,
    new_w_ref, new_state_ref,
    order_ref, grad_ref, ids_ref, len_ref, w_ref, state_ref,
    send_grad, recv_grad, send_ids, all_ids, acc, own_square, pair_square, squares,
    in_sem, gs_sem, gr_sem, is_sem, ir_sem, cs_sem, cr_sem, ks_sem, kr_sem, qs_sem, qr_sem,
):
    t = lax.axis_index("table")
    c = lax.axis_index("col")
    slots, dim, rows = w_ref.shape
    samples = grad_ref.shape[2]
    highs = rows // LOW
    across = 4 if tables % 4 == 0 else 1
    deep = tables // across
    shares = tables // cols
    chips = cols // 2
    z, x = t // across, t % across
    y, core = c // 2, c % 2
    mate = (t, y * 2 + (1 - core))

    def wrap(value, size):
        return jnp.where(value >= size, value - size, value)

    def beside(dx, sign):
        return wrap(x + (dx if sign > 0 else across - dx), across)

    def above(q, sign):
        far = (q + 1) // 2
        ahead = (q % 2 == 1) if sign > 0 else (q % 2 == 0)
        return wrap(z + jnp.where(ahead, far, deep - far), deep)

    def each_partner(sign, visit):
        line = [beside(dx, sign) for dx in range(across)]
        for dx in range(1, across):
            visit(z * across + line[dx])

        @pl.loop(0, deep - 1)
        def _(step):
            base = above(step + 1, sign) * across
            for dx in range(across):
                visit(base + line[dx])

    def chip_peer(step):
        return wrap(y + step, chips)

    loads = [
        pltpu.make_async_copy(src, dst, in_sem.at[n])
        for n, (src, dst) in enumerate((
            (order_hbm, order_ref), (grad_hbm, grad_ref), (len_hbm, len_ref),
            (ids_hbm, ids_ref), (w_hbm, w_ref), (state_hbm, state_ref),
        ))
    ]
    for load in loads:
        load.start()

    barrier = pltpu.get_barrier_semaphore()
    pl.semaphore_signal(barrier, inc=1, device_id=mate, device_id_type=MESH)

    @pl.loop(1, chips)
    def _(step):
        pl.semaphore_signal(barrier, inc=1, device_id=(t, chip_peer(step) * 2 + core), device_id_type=MESH)

    loads[0].wait()
    loads[1].wait()

    def greet(target):
        pl.semaphore_signal(barrier, inc=1, device_id=(target, c), device_id_type=MESH)
        for slot in range(slots):
            send_grad[target, slot] = grad_ref[order_ref[slots * target + slot]]

    each_partner(1, greet)
    for slot in range(slots):
        recv_grad[t, slot] = grad_ref[order_ref[slots * t + slot]]

    loads[2].wait()
    loads[3].wait()
    place = lax.broadcasted_iota(jnp.int32, (place_count, samples), 0)

    def ids_target(share):
        return (c - t % cols + cols) % cols + cols * share

    for share in range(shares):
        target = ids_target(share)
        live = []
        for slot in range(slots):
            feature = order_ref[slots * target + slot]
            length = len_ref[pl.ds(feature, 1), :]
            live.append(jnp.where(place < length, ids_ref[feature], -1))
        send_ids[share] = jnp.concatenate(live, axis=0)
    acc[...] = jnp.zeros_like(acc)

    pl.semaphore_wait(barrier, tables - 1 + chips - 1 + 1)

    own_ids = all_ids.at[core, y]

    def ids_copy(share, landing):
        return pltpu.make_async_remote_copy(
            src_ref=send_ids.at[share],
            dst_ref=own_ids.at[landing],
            send_sem=is_sem.at[share],
            recv_sem=ir_sem.at[landing],
            device_id=(ids_target(share), c),
            device_id_type=MESH,
        )

    for share in range(shares):
        @pl.when(ids_target(share) == t)
        def _():
            all_ids[core, y, t // cols] = send_ids[share]

        @pl.when(ids_target(share) != t)
        def _():
            ids_copy(share, t // cols).start()

    def grad_copy(target, source):
        return pltpu.make_async_remote_copy(
            src_ref=send_grad.at[target],
            dst_ref=recv_grad.at[source],
            send_sem=gs_sem.at[target],
            recv_sem=gr_sem.at[source],
            device_id=(target, c),
            device_id_type=MESH,
        )

    each_partner(1, lambda target: grad_copy(target, t).start())

    for share in range(shares):
        @pl.when(ids_target(share) != t)
        def _():
            ids_copy(share, share).wait_recv()

    def chip_ids(peer, owner):
        return pltpu.make_async_remote_copy(
            src_ref=all_ids.at[core, owner],
            dst_ref=all_ids.at[core, owner],
            send_sem=cs_sem.at[peer],
            recv_sem=cr_sem.at[owner],
            device_id=(t, peer * 2 + core),
            device_id_type=MESH,
        )

    @pl.loop(1, chips)
    def _(step):
        chip_ids(chip_peer(step), y).start()

    @pl.loop(1, chips)
    def _(step):
        peer = chip_peer(step)
        chip_ids(peer, peer).wait_recv()

    def mate_ids(owner):
        return pltpu.make_async_remote_copy(
            src_ref=all_ids.at[owner],
            dst_ref=all_ids.at[owner],
            send_sem=ks_sem.at[0],
            recv_sem=kr_sem.at[0],
            device_id=mate,
            device_id_type=MESH,
        )

    mate_ids(core).start()
    mate_ids(1 - core).wait_recv()

    low_line = lax.broadcasted_iota(jnp.int32, (LOW, samples), 0).astype(jnp.float32).astype(jnp.bfloat16)
    one, none = jnp.bfloat16(1.0), jnp.bfloat16(0.0)

    def work(source):
        holder = (source + t) % cols
        block = all_ids[holder % 2, holder // 2, source // cols]
        high = (block >> 8).astype(jnp.float32).astype(jnp.bfloat16)
        low = (block & (LOW - 1)).astype(jnp.float32).astype(jnp.bfloat16)
        for slot in range(slots):
            grad = recv_grad[source, slot]
            left, right = [], []
            for p in range(place_count):
                row = slot * place_count + p
                low_row = jnp.broadcast_to(low[row:row + 1], (LOW, samples))
                right.append(jnp.where(low_row == low_line, one, none))
                high_row = jnp.broadcast_to(high[row:row + 1], (dim, samples))
                left.append(jnp.concatenate(
                    [jnp.where(high_row == jnp.bfloat16(h), grad, none) for h in range(highs)], axis=0))
            acc[slot] += lax.dot_general(
                jnp.concatenate(left, axis=1), jnp.concatenate(right, axis=1),
                (((1,), (1,)), ((), ())), preferred_element_type=jnp.float32)

    work(t)

    @pl.loop(1, tables)
    def _(step):
        turned = jnp.where(step >= tables, step - tables + 1, step)
        q = jnp.where(step >= tables, 0, step // across)
        source = above(q, -1) * across + wrap(x + across - turned % across, across)
        grad_copy(source, source).wait_recv()
        work(source)

    loads[4].wait()
    loads[5].wait()
    sums = []
    for slot in range(slots):
        for h in range(highs):
            part = acc[slot, h * dim:(h + 1) * dim, :]
            sums.append(jnp.sum(part * part, axis=0, keepdims=True))
    own_square[...] = jnp.concatenate(sums, axis=0)

    mate_square = pltpu.make_async_remote_copy(
        src_ref=own_square,
        dst_ref=pair_square,
        send_sem=ks_sem.at[1],
        recv_sem=kr_sem.at[1],
        device_id=mate,
        device_id_type=MESH,
    )
    mate_square.start()
    mate_square.wait_recv()
    squares[y] = own_square[...] + pair_square[...]

    def square_copy(peer, owner):
        return pltpu.make_async_remote_copy(
            src_ref=squares.at[owner],
            dst_ref=squares.at[owner],
            send_sem=qs_sem.at[peer],
            recv_sem=qr_sem.at[owner],
            device_id=(t, peer * 2 + core),
            device_id_type=MESH,
        )

    for step in range(1, chips):
        square_copy(chip_peer(step), y).start()

    for step in range(1, chips):
        peer = chip_peer(step)
        square_copy(peer, peer).wait_recv()

    total = squares[0]
    for peer in range(1, chips):
        total = total + squares[peer]
    full = dim * cols
    for slot in range(slots):
        for h in range(highs):
            row = slot * highs + h
            span = slice(h * LOW, (h + 1) * LOW)
            new_state = state_ref[slot:slot + 1, span] + total[row:row + 1] / full
            new_state_ref[slot:slot + 1, span] = new_state
            scale = 0.3 / jnp.sqrt(new_state)
            new_w_ref[slot, :, span] = w_ref[slot, :, span] - acc[slot, h * dim:(h + 1) * dim, :] * scale

    for share in range(shares):
        @pl.when(ids_target(share) != t)
        def _():
            ids_copy(share, t // cols).wait_send()

    mate_ids(core).wait_send()
    mate_square.wait_send()

    @pl.loop(1, chips)
    def _(step):
        peer = chip_peer(step)
        chip_ids(peer, y).wait_send()
        square_copy(peer, y).wait_send()

    each_partner(1, lambda target: grad_copy(target, t).wait_send())


def solution(mesh):
    tables, cols = mesh.shape["table"], mesh.shape["col"]

    def body(pooled_grad, row_ids, lengths, feature_order, weights, state):
        features, width, samples = pooled_grad.shape
        place_count = row_ids.shape[1]
        slots, dim, rows = weights.shape
        shares = tables // cols
        vmem = pl.BlockSpec(memory_space=pltpu.VMEM)
        dma = pltpu.SemaphoreType.DMA
        chips = cols // 2
        block = slots * place_count
        squares = (slots * (rows // LOW), LOW)
        return pl.pallas_call(
            functools.partial(kernel, tables, cols, place_count),
            out_shape=(
                jax.ShapeDtypeStruct(weights.shape, jnp.float32),
                jax.ShapeDtypeStruct(state.shape, jnp.float32),
            ),
            in_specs=[pl.BlockSpec(memory_space=pltpu.HBM)] * 6,
            out_specs=(vmem, vmem),
            scratch_shapes=[
                pltpu.SMEM(feature_order.shape, jnp.int32),
                pltpu.VMEM(pooled_grad.shape, jnp.bfloat16),
                pltpu.VMEM(row_ids.shape, jnp.int32),
                pltpu.VMEM(lengths.shape, jnp.int32),
                pltpu.VMEM(weights.shape, jnp.float32),
                pltpu.VMEM(state.shape, jnp.float32),
                pltpu.VMEM((tables, slots, dim, samples), jnp.bfloat16),
                pltpu.VMEM((tables, slots, dim, samples), jnp.bfloat16),
                pltpu.VMEM((shares, block, samples), jnp.int32),
                pltpu.VMEM((2, chips, shares, block, samples), jnp.int32),
                pltpu.VMEM((slots, rows // LOW * dim, LOW), jnp.float32),
                pltpu.VMEM(squares, jnp.float32),
                pltpu.VMEM(squares, jnp.float32),
                pltpu.VMEM((chips,) + squares, jnp.float32),
                dma((6,)),
                dma((tables,)), dma((tables,)),
                dma((shares,)), dma((shares,)),
                dma((chips,)), dma((chips,)),
                dma((2,)), dma((2,)),
                dma((chips,)), dma((chips,)),
            ],
            compiler_params=pltpu.CompilerParams(
                collective_id=0, has_side_effects=True, vmem_limit_bytes=60 * 1024 * 1024
            ),
            cost_estimate=pl.CostEstimate(
                flops=4 * slots * tables * samples * rows * dim, bytes_accessed=4 * 1024 * 1024, transcendentals=0
            ),
        )(feature_order, pooled_grad, row_ids, lengths, weights, state)

    return jax.shard_map(
        body,
        mesh=mesh,
        in_specs=(
            P(None, "col", "table"),
            P(None, None, "table"),
            P(None, "table"),
            P(),
            P("table", "col", None),
            P("table", None),
        ),
        out_specs=(P("table", "col", None), P("table", None)),
        check_vma=False,
    )
```

```python
import functools

import jax
import jax.numpy as jnp
from jax import lax
from jax.experimental import pallas as pl
from jax.experimental.pallas import tpu as pltpu
from jax.sharding import PartitionSpec as P

MESH = pl.DeviceIdType.MESH
LOW = 256
DEEP = 12
REACH = 4
STEP = 2


def kernel(
    tables, cols, place_count, order_hbm, grad_hbm, ids_hbm, len_hbm, w_hbm, state_hbm,
    new_w_ref, new_state_ref,
    order_ref, grad_ref, ids_ref, len_ref, w_ref, state_ref,
    send_grad, recv_grad, send_ids, all_ids, acc, partial, own_square, pair_square, squares,
    in_sem, gs_sem, gr_sem, is_sem, ir_sem, cs_sem, cr_sem, ks_sem, kr_sem, qs_sem, qr_sem, ps_sem, pr_sem,
):
    t = lax.axis_index("table")
    c = lax.axis_index("col")
    slots, dim, rows = w_ref.shape
    samples = grad_ref.shape[2]
    highs = rows // LOW
    deep = DEEP
    across = tables // deep
    shares = tables // cols
    chips = cols // 2
    far_blocks = 9 * across
    z, x = t // across, t % across
    y, core = c // 2, c % 2
    mate = (t, y * 2 + (1 - core))

    def wrap(value, size):
        return jnp.where(value >= size, value - size, jnp.where(value < 0, value + size, value))

    def route(block):
        q, dx = block // across, block % across
        ahead = jnp.where(q == 0, dx % 2 == 0, q % 2 == 1)
        far = q <= 8
        reach = jnp.where(q == 0, 4, jnp.where(far, (8 - q) // 2, (12 - q) // 2))
        source = jnp.where(ahead, reach, -reach)
        owner = jnp.where(far, jnp.where(ahead, -STEP, STEP), 0)
        role = jnp.where(far, jnp.where(ahead, 1, 2), 0)
        return source, dx, owner, role

    def send_to(block):
        source, dx, owner, _ = route(block)
        home = wrap(x - dx, across)
        at = wrap(z - source, deep)
        return at * across + home, wrap(at + owner, deep) * across + home

    def chip_peer(step):
        return wrap(y + step, chips)

    loads = [
        pltpu.make_async_copy(src, dst, in_sem.at[n])
        for n, (src, dst) in enumerate((
            (order_hbm, order_ref), (grad_hbm, grad_ref), (len_hbm, len_ref),
            (ids_hbm, ids_ref), (w_hbm, w_ref), (state_hbm, state_ref),
        ))
    ]
    for load in loads:
        load.start()

    barrier = pltpu.get_barrier_semaphore()
    pl.semaphore_signal(barrier, inc=1, device_id=mate, device_id_type=MESH)

    @pl.loop(1, chips)
    def _(step):
        pl.semaphore_signal(barrier, inc=1, device_id=(t, chip_peer(step) * 2 + core), device_id_type=MESH)

    for dx in range(1, across):
        pl.semaphore_signal(barrier, inc=1, device_id=(z * across + wrap(x + dx, across), c), device_id_type=MESH)

    @pl.loop(1, 2 * REACH + 1)
    def _(step):
        plane = wrap(z + jnp.where(step > REACH, REACH - step, step), deep) * across
        for dx in range(across):
            pl.semaphore_signal(barrier, inc=1, device_id=(plane + wrap(x + dx, across), c), device_id_type=MESH)

    loads[0].wait()
    loads[1].wait()

    @pl.loop(0, tables)
    def _(block):
        target, owner = send_to(block)

        @pl.when(target == t)
        def _():
            for slot in range(slots):
                recv_grad[slot, block] = grad_ref[order_ref[slots * owner + slot]]

        @pl.when(target != t)
        def _():
            for slot in range(slots):
                send_grad[slot, block] = grad_ref[order_ref[slots * owner + slot]]

    loads[2].wait()
    loads[3].wait()
    place = lax.broadcasted_iota(jnp.int32, (place_count, samples), 0)
    for share in range(shares):
        _, owner = send_to(c + cols * share)
        live = []
        for slot in range(slots):
            feature = order_ref[slots * owner + slot]
            length = len_ref[pl.ds(feature, 1), :]
            live.append(jnp.where(place < length, ids_ref[feature], -1))
        send_ids[share] = jnp.concatenate(live, axis=0)
    acc[...] = jnp.zeros_like(acc)

    pl.semaphore_wait(barrier, (2 * REACH + 1) * across - 1 + chips - 1 + 1)

    def ids_copy(share):
        return pltpu.make_async_remote_copy(
            src_ref=send_ids.at[share],
            dst_ref=all_ids.at[core, y, share],
            send_sem=is_sem.at[share],
            recv_sem=ir_sem.at[share],
            device_id=(send_to(c + cols * share)[0], c),
            device_id_type=MESH,
        )

    def own_share(share):
        return send_to(c + cols * share)[0] == t

    for share in range(shares):
        @pl.when(own_share(share))
        def _():
            all_ids[core, y, share] = send_ids[share]

        @pl.when(jnp.logical_not(own_share(share)))
        def _():
            ids_copy(share).start()

    def grad_copy(slot, block, target):
        return pltpu.make_async_remote_copy(
            src_ref=send_grad.at[slot, block],
            dst_ref=recv_grad.at[slot, block],
            send_sem=gs_sem.at[slot, block],
            recv_sem=gr_sem.at[slot, block],
            device_id=(target, c),
            device_id_type=MESH,
        )

    def send_blocks(slot, first, last):
        @pl.loop(first, last)
        def _(block):
            target, _ = send_to(block)

            @pl.when(target != t)
            def _():
                grad_copy(slot, block, target).start()

    for slot in range(slots):
        send_blocks(slot, 0, far_blocks)
    for slot in range(slots):
        send_blocks(slot, far_blocks, tables)

    for share in range(shares):
        @pl.when(jnp.logical_not(own_share(share)))
        def _():
            ids_copy(share).wait_recv()

    def chip_ids(peer, owner):
        return pltpu.make_async_remote_copy(
            src_ref=all_ids.at[core, owner],
            dst_ref=all_ids.at[core, owner],
            send_sem=cs_sem.at[peer],
            recv_sem=cr_sem.at[owner],
            device_id=(t, peer * 2 + core),
            device_id_type=MESH,
        )

    @pl.loop(1, chips)
    def _(step):
        chip_ids(chip_peer(step), y).start()

    @pl.loop(1, chips)
    def _(step):
        peer = chip_peer(step)
        chip_ids(peer, peer).wait_recv()

    def mate_ids(owner):
        return pltpu.make_async_remote_copy(
            src_ref=all_ids.at[owner],
            dst_ref=all_ids.at[owner],
            send_sem=ks_sem.at[0],
            recv_sem=kr_sem.at[0],
            device_id=mate,
            device_id_type=MESH,
        )

    mate_ids(core).start()
    mate_ids(1 - core).wait_recv()

    low_line = lax.broadcasted_iota(jnp.int32, (LOW, samples), 0).astype(jnp.float32).astype(jnp.bfloat16)
    one, none = jnp.bfloat16(1.0), jnp.bfloat16(0.0)

    def work(slot, blocks):
        left, right = [], []
        for block in blocks:
            holder = block % cols
            ids = all_ids[holder % 2, holder // 2, block // cols]
            high = (ids >> 8).astype(jnp.float32).astype(jnp.bfloat16)
            low = (ids & (LOW - 1)).astype(jnp.float32).astype(jnp.bfloat16)
            grad = recv_grad[slot, block]
            for p in range(place_count):
                row = slot * place_count + p
                low_row = jnp.broadcast_to(low[row:row + 1], (LOW, samples))
                right.append(jnp.where(low_row == low_line, one, none))
                high_row = jnp.broadcast_to(high[row:row + 1], (dim, samples))
                left.append(jnp.concatenate(
                    [jnp.where(high_row == jnp.bfloat16(h), grad, none) for h in range(highs)], axis=0))
        role = route(blocks[0])[3]
        acc[role, slot] += lax.dot_general(
            jnp.concatenate(left, axis=1), jnp.concatenate(right, axis=1),
            (((1,), (1,)), ((), ())), preferred_element_type=jnp.float32)

    groups = [(0, 2), (1, 3)] if across == 4 else [(dx,) for dx in range(across)]

    def work_blocks(slot, first, last):
        @pl.loop(first // across, last // across)
        def _(q):
            for group in groups:
                blocks = [q * across + dx for dx in group]
                for block in blocks:
                    target, _ = send_to(block)

                    @pl.when(target != t)
                    def _():
                        grad_copy(slot, block, target).wait_recv()
                work(slot, blocks)

    def partial_copy(slot, side):
        return pltpu.make_async_remote_copy(
            src_ref=acc.at[1 + side, slot],
            dst_ref=partial.at[side, slot],
            send_sem=ps_sem.at[side, slot],
            recv_sem=pr_sem.at[side, slot],
            device_id=(wrap(z + (STEP if side else -STEP), deep) * across + x, c),
            device_id_type=MESH,
        )

    for slot in range(slots):
        work_blocks(slot, 0, far_blocks)
        for side in range(2):
            partial_copy(slot, side).start()
    for slot in range(slots):
        work_blocks(slot, far_blocks, tables)

    loads[4].wait()
    loads[5].wait()
    sums = []
    for slot in range(slots):
        for side in range(2):
            partial_copy(slot, side).wait_recv()
        for h in range(highs):
            part = slice(h * dim, (h + 1) * dim)
            total = acc[0, slot, part, :] + partial[0, slot, part, :] + partial[1, slot, part, :]
            acc[0, slot, part, :] = total
            sums.append(jnp.sum(total * total, axis=0, keepdims=True))
    own_square[...] = jnp.concatenate(sums, axis=0)

    mate_square = pltpu.make_async_remote_copy(
        src_ref=own_square,
        dst_ref=pair_square,
        send_sem=ks_sem.at[1],
        recv_sem=kr_sem.at[1],
        device_id=mate,
        device_id_type=MESH,
    )
    mate_square.start()
    mate_square.wait_recv()
    squares[y] = own_square[...] + pair_square[...]

    def square_copy(peer, owner):
        return pltpu.make_async_remote_copy(
            src_ref=squares.at[owner],
            dst_ref=squares.at[owner],
            send_sem=qs_sem.at[peer],
            recv_sem=qr_sem.at[owner],
            device_id=(t, peer * 2 + core),
            device_id_type=MESH,
        )

    for step in range(1, chips):
        square_copy(chip_peer(step), y).start()

    for step in range(1, chips):
        peer = chip_peer(step)
        square_copy(peer, peer).wait_recv()

    total = squares[0]
    for peer in range(1, chips):
        total = total + squares[peer]
    full = dim * cols
    for slot in range(slots):
        for h in range(highs):
            row = slot * highs + h
            span = slice(h * LOW, (h + 1) * LOW)
            new_state = state_ref[slot:slot + 1, span] + total[row:row + 1] / full
            new_state_ref[slot:slot + 1, span] = new_state
            scale = 0.3 / jnp.sqrt(new_state)
            new_w_ref[slot, :, span] = w_ref[slot, :, span] - acc[0, slot, h * dim:(h + 1) * dim, :] * scale

    for share in range(shares):
        @pl.when(jnp.logical_not(own_share(share)))
        def _():
            ids_copy(share).wait_send()

    mate_ids(core).wait_send()
    mate_square.wait_send()

    @pl.loop(1, chips)
    def _(step):
        peer = chip_peer(step)
        chip_ids(peer, y).wait_send()
        square_copy(peer, y).wait_send()

    for slot in range(slots):
        for side in range(2):
            partial_copy(slot, side).wait_send()

    @pl.loop(0, tables)
    def _(block):
        target, _ = send_to(block)

        @pl.when(target != t)
        def _():
            for slot in range(slots):
                grad_copy(slot, block, target).wait_send()


def solution(mesh):
    tables, cols = mesh.shape["table"], mesh.shape["col"]

    def body(pooled_grad, row_ids, lengths, feature_order, weights, state):
        features, width, samples = pooled_grad.shape
        place_count = row_ids.shape[1]
        slots, dim, rows = weights.shape
        shares = tables // cols
        vmem = pl.BlockSpec(memory_space=pltpu.VMEM)
        dma = pltpu.SemaphoreType.DMA
        chips = cols // 2
        block = slots * place_count
        squares = (slots * (rows // LOW), LOW)
        return pl.pallas_call(
            functools.partial(kernel, tables, cols, place_count),
            out_shape=(
                jax.ShapeDtypeStruct(weights.shape, jnp.float32),
                jax.ShapeDtypeStruct(state.shape, jnp.float32),
            ),
            in_specs=[pl.BlockSpec(memory_space=pltpu.HBM)] * 6,
            out_specs=(vmem, vmem),
            scratch_shapes=[
                pltpu.SMEM(feature_order.shape, jnp.int32),
                pltpu.VMEM(pooled_grad.shape, jnp.bfloat16),
                pltpu.VMEM(row_ids.shape, jnp.int32),
                pltpu.VMEM(lengths.shape, jnp.int32),
                pltpu.VMEM(weights.shape, jnp.float32),
                pltpu.VMEM(state.shape, jnp.float32),
                pltpu.VMEM((slots, tables, dim, samples), jnp.bfloat16),
                pltpu.VMEM((slots, tables, dim, samples), jnp.bfloat16),
                pltpu.VMEM((shares, block, samples), jnp.int32),
                pltpu.VMEM((2, chips, shares, block, samples), jnp.int32),
                pltpu.VMEM((3, slots, rows // LOW * dim, LOW), jnp.float32),
                pltpu.VMEM((2, slots, rows // LOW * dim, LOW), jnp.float32),
                pltpu.VMEM(squares, jnp.float32),
                pltpu.VMEM(squares, jnp.float32),
                pltpu.VMEM((chips,) + squares, jnp.float32),
                dma((6,)),
                dma((slots, tables)), dma((slots, tables)),
                dma((shares,)), dma((shares,)),
                dma((chips,)), dma((chips,)),
                dma((2,)), dma((2,)),
                dma((chips,)), dma((chips,)),
                dma((2, slots)), dma((2, slots)),
            ],
            compiler_params=pltpu.CompilerParams(
                collective_id=0, has_side_effects=True, vmem_limit_bytes=60 * 1024 * 1024
            ),
            cost_estimate=pl.CostEstimate(
                flops=4 * slots * tables * samples * rows * dim, bytes_accessed=4 * 1024 * 1024, transcendentals=0
            ),
        )(feature_order, pooled_grad, row_ids, lengths, weights, state)

    return jax.shard_map(
        body,
        mesh=mesh,
        in_specs=(
            P(None, "col", "table"),
            P(None, None, "table"),
            P(None, "table"),
            P(),
            P("table", "col", None),
            P("table", None),
        ),
        out_specs=(P("table", "col", None), P("table", None)),
        check_vma=False,
    )
```

```python
import functools

import jax
import jax.numpy as jnp
from jax import lax
from jax.experimental import pallas as pl
from jax.experimental.pallas import tpu as pltpu
from jax.sharding import PartitionSpec as P

MESH = pl.DeviceIdType.MESH
LOW = 128
DEEP = 12
REACH = 4
STEP = 2


def kernel(
    tables, cols, place_count, order_hbm, grad_hbm, ids_hbm, len_hbm, w_hbm, state_hbm,
    new_w_ref, new_state_ref,
    order_ref, grad_ref, ids_ref, len_ref, w_ref, state_ref,
    send_grad, recv_grad, send_ids, all_ids, acc, partial, own_square, pair_square, squares,
    in_sem, gs_sem, gr_sem, is_sem, ir_sem, cs_sem, cr_sem, ks_sem, kr_sem, qs_sem, qr_sem, ps_sem, pr_sem,
):
    t = lax.axis_index("table")
    c = lax.axis_index("col")
    slots, dim, rows = w_ref.shape
    samples = grad_ref.shape[2]
    highs = rows // LOW
    deep = DEEP
    across = tables // deep
    shares = tables // cols
    chips = cols // 2
    far_blocks = 9 * across
    z, x = t // across, t % across
    y, core = c // 2, c % 2
    mate = (t, y * 2 + (1 - core))

    def wrap(value, size):
        return jnp.where(value >= size, value - size, jnp.where(value < 0, value + size, value))

    def route(block):
        q, dx = block // across, block % across
        ahead = jnp.where(q == 0, dx % 2 == 0, q % 2 == 1)
        far = q <= 8
        reach = jnp.where(q == 0, 4, jnp.where(far, (8 - q) // 2, (12 - q) // 2))
        source = jnp.where(ahead, reach, -reach)
        owner = jnp.where(far, jnp.where(ahead, -STEP, STEP), 0)
        role = jnp.where(far, jnp.where(ahead, 1, 2), 0)
        return source, dx, owner, role

    def send_to(block):
        source, dx, owner, _ = route(block)
        home = wrap(x - dx, across)
        at = wrap(z - source, deep)
        return at * across + home, wrap(at + owner, deep) * across + home

    def chip_peer(step):
        return wrap(y + step, chips)

    loads = [
        pltpu.make_async_copy(src, dst, in_sem.at[n])
        for n, (src, dst) in enumerate((
            (order_hbm, order_ref), (grad_hbm, grad_ref), (len_hbm, len_ref),
            (ids_hbm, ids_ref), (w_hbm, w_ref), (state_hbm, state_ref),
        ))
    ]
    for load in loads:
        load.start()

    barrier = pltpu.get_barrier_semaphore()
    pl.semaphore_signal(barrier, inc=1, device_id=mate, device_id_type=MESH)

    @pl.loop(1, chips)
    def _(step):
        pl.semaphore_signal(barrier, inc=1, device_id=(t, chip_peer(step) * 2 + core), device_id_type=MESH)

    for dx in range(1, across):
        pl.semaphore_signal(barrier, inc=1, device_id=(z * across + wrap(x + dx, across), c), device_id_type=MESH)

    @pl.loop(1, 2 * REACH + 1)
    def _(step):
        plane = wrap(z + jnp.where(step > REACH, REACH - step, step), deep) * across
        for dx in range(across):
            pl.semaphore_signal(barrier, inc=1, device_id=(plane + wrap(x + dx, across), c), device_id_type=MESH)

    loads[0].wait()
    loads[1].wait()

    @pl.loop(0, tables)
    def _(block):
        target, owner = send_to(block)

        @pl.when(target == t)
        def _():
            for slot in range(slots):
                recv_grad[slot, block] = grad_ref[order_ref[slots * owner + slot]]

        @pl.when(target != t)
        def _():
            for slot in range(slots):
                send_grad[slot, block] = grad_ref[order_ref[slots * owner + slot]]

    loads[2].wait()
    loads[3].wait()
    place = lax.broadcasted_iota(jnp.int32, (place_count, samples), 0)
    for share in range(shares):
        _, owner = send_to(c + cols * share)
        live = []
        for slot in range(slots):
            feature = order_ref[slots * owner + slot]
            length = len_ref[pl.ds(feature, 1), :]
            live.append(jnp.where(place < length, ids_ref[feature], -1))
        send_ids[share] = jnp.concatenate(live, axis=0)
    acc[...] = jnp.zeros_like(acc)

    pl.semaphore_wait(barrier, (2 * REACH + 1) * across - 1 + chips - 1 + 1)

    def ids_copy(share):
        return pltpu.make_async_remote_copy(
            src_ref=send_ids.at[share],
            dst_ref=all_ids.at[core, y, share],
            send_sem=is_sem.at[share],
            recv_sem=ir_sem.at[share],
            device_id=(send_to(c + cols * share)[0], c),
            device_id_type=MESH,
        )

    def own_share(share):
        return send_to(c + cols * share)[0] == t

    for share in range(shares):
        @pl.when(own_share(share))
        def _():
            all_ids[core, y, share] = send_ids[share]

        @pl.when(jnp.logical_not(own_share(share)))
        def _():
            ids_copy(share).start()

    def grad_copy(slot, block, target):
        return pltpu.make_async_remote_copy(
            src_ref=send_grad.at[slot, block],
            dst_ref=recv_grad.at[slot, block],
            send_sem=gs_sem.at[slot, block],
            recv_sem=gr_sem.at[slot, block],
            device_id=(target, c),
            device_id_type=MESH,
        )

    def send_blocks(slot, first, last):
        @pl.loop(first, last)
        def _(block):
            target, _ = send_to(block)

            @pl.when(target != t)
            def _():
                grad_copy(slot, block, target).start()

    for slot in range(slots):
        send_blocks(slot, 0, far_blocks)
    for slot in range(slots):
        send_blocks(slot, far_blocks, tables)

    for share in range(shares):
        @pl.when(jnp.logical_not(own_share(share)))
        def _():
            ids_copy(share).wait_recv()

    def chip_ids(peer, owner):
        return pltpu.make_async_remote_copy(
            src_ref=all_ids.at[core, owner],
            dst_ref=all_ids.at[core, owner],
            send_sem=cs_sem.at[peer],
            recv_sem=cr_sem.at[owner],
            device_id=(t, peer * 2 + core),
            device_id_type=MESH,
        )

    @pl.loop(1, chips)
    def _(step):
        chip_ids(chip_peer(step), y).start()

    @pl.loop(1, chips)
    def _(step):
        peer = chip_peer(step)
        chip_ids(peer, peer).wait_recv()

    def mate_ids(owner):
        return pltpu.make_async_remote_copy(
            src_ref=all_ids.at[owner],
            dst_ref=all_ids.at[owner],
            send_sem=ks_sem.at[0],
            recv_sem=kr_sem.at[0],
            device_id=mate,
            device_id_type=MESH,
        )

    mate_ids(core).start()
    mate_ids(1 - core).wait_recv()

    low_line = lax.broadcasted_iota(jnp.int32, (LOW, samples), 0).astype(jnp.float32).astype(jnp.bfloat16)
    one, none = jnp.bfloat16(1.0), jnp.bfloat16(0.0)

    def work(slot, blocks):
        left, right = [], []
        for block in blocks:
            holder = block % cols
            ids = all_ids[holder % 2, holder // 2, block // cols]
            high = (ids >> (LOW.bit_length() - 1)).astype(jnp.float32).astype(jnp.bfloat16)
            low = (ids & (LOW - 1)).astype(jnp.float32).astype(jnp.bfloat16)
            grad = recv_grad[slot, block]
            for p in range(place_count):
                row = slot * place_count + p
                low_row = jnp.broadcast_to(low[row:row + 1], (LOW, samples))
                right.append(jnp.where(low_row == low_line, one, none))
                high_row = jnp.broadcast_to(high[row:row + 1], (dim, samples))
                left.append(jnp.concatenate(
                    [jnp.where(high_row == jnp.bfloat16(h), grad, none) for h in range(highs)], axis=0))
        role = route(blocks[0])[3]
        acc[role, slot] += lax.dot_general(
            jnp.concatenate(left, axis=1), jnp.concatenate(right, axis=1),
            (((1,), (1,)), ((), ())), preferred_element_type=jnp.float32)

    groups = [(0, 2), (1, 3)] if across == 4 else [(dx,) for dx in range(across)]

    def work_blocks(slot, first, last):
        @pl.loop(first // across, last // across)
        def _(q):
            for group in groups:
                blocks = [q * across + dx for dx in group]
                for block in blocks:
                    target, _ = send_to(block)

                    @pl.when(target != t)
                    def _():
                        grad_copy(slot, block, target).wait_recv()
                work(slot, blocks)

    def partial_copy(slot, side):
        return pltpu.make_async_remote_copy(
            src_ref=acc.at[1 + side, slot],
            dst_ref=partial.at[side, slot],
            send_sem=ps_sem.at[side, slot],
            recv_sem=pr_sem.at[side, slot],
            device_id=(wrap(z + (STEP if side else -STEP), deep) * across + x, c),
            device_id_type=MESH,
        )

    for slot in range(slots):
        work_blocks(slot, 0, far_blocks)
        for side in range(2):
            partial_copy(slot, side).start()
    for slot in range(slots):
        work_blocks(slot, far_blocks, tables)

    loads[4].wait()
    loads[5].wait()
    sums = []
    for slot in range(slots):
        for side in range(2):
            partial_copy(slot, side).wait_recv()
        for h in range(highs):
            part = slice(h * dim, (h + 1) * dim)
            total = acc[0, slot, part, :] + partial[0, slot, part, :] + partial[1, slot, part, :]
            acc[0, slot, part, :] = total
            sums.append(jnp.sum(total * total, axis=0, keepdims=True))
    own_square[...] = jnp.concatenate(sums, axis=0)

    mate_square = pltpu.make_async_remote_copy(
        src_ref=own_square,
        dst_ref=pair_square,
        send_sem=ks_sem.at[1],
        recv_sem=kr_sem.at[1],
        device_id=mate,
        device_id_type=MESH,
    )
    mate_square.start()
    mate_square.wait_recv()
    squares[y] = own_square[...] + pair_square[...]

    def square_copy(peer, owner):
        return pltpu.make_async_remote_copy(
            src_ref=squares.at[owner],
            dst_ref=squares.at[owner],
            send_sem=qs_sem.at[peer],
            recv_sem=qr_sem.at[owner],
            device_id=(t, peer * 2 + core),
            device_id_type=MESH,
        )

    for step in range(1, chips):
        square_copy(chip_peer(step), y).start()

    for step in range(1, chips):
        peer = chip_peer(step)
        square_copy(peer, peer).wait_recv()

    total = squares[0]
    for peer in range(1, chips):
        total = total + squares[peer]
    full = dim * cols
    for slot in range(slots):
        for h in range(highs):
            row = slot * highs + h
            span = slice(h * LOW, (h + 1) * LOW)
            new_state = state_ref[slot:slot + 1, span] + total[row:row + 1] / full
            new_state_ref[slot:slot + 1, span] = new_state
            scale = 0.3 / jnp.sqrt(new_state)
            new_w_ref[slot, :, span] = w_ref[slot, :, span] - acc[0, slot, h * dim:(h + 1) * dim, :] * scale

    for share in range(shares):
        @pl.when(jnp.logical_not(own_share(share)))
        def _():
            ids_copy(share).wait_send()

    mate_ids(core).wait_send()
    mate_square.wait_send()

    @pl.loop(1, chips)
    def _(step):
        peer = chip_peer(step)
        chip_ids(peer, y).wait_send()
        square_copy(peer, y).wait_send()

    for slot in range(slots):
        for side in range(2):
            partial_copy(slot, side).wait_send()

    @pl.loop(0, tables)
    def _(block):
        target, _ = send_to(block)

        @pl.when(target != t)
        def _():
            for slot in range(slots):
                grad_copy(slot, block, target).wait_send()


def solution(mesh):
    tables, cols = mesh.shape["table"], mesh.shape["col"]

    def body(pooled_grad, row_ids, lengths, feature_order, weights, state):
        features, width, samples = pooled_grad.shape
        place_count = row_ids.shape[1]
        slots, dim, rows = weights.shape
        shares = tables // cols
        vmem = pl.BlockSpec(memory_space=pltpu.VMEM)
        dma = pltpu.SemaphoreType.DMA
        chips = cols // 2
        block = slots * place_count
        squares = (slots * (rows // LOW), LOW)
        return pl.pallas_call(
            functools.partial(kernel, tables, cols, place_count),
            out_shape=(
                jax.ShapeDtypeStruct(weights.shape, jnp.float32),
                jax.ShapeDtypeStruct(state.shape, jnp.float32),
            ),
            in_specs=[pl.BlockSpec(memory_space=pltpu.HBM)] * 6,
            out_specs=(vmem, vmem),
            scratch_shapes=[
                pltpu.SMEM(feature_order.shape, jnp.int32),
                pltpu.VMEM(pooled_grad.shape, jnp.bfloat16),
                pltpu.VMEM(row_ids.shape, jnp.int32),
                pltpu.VMEM(lengths.shape, jnp.int32),
                pltpu.VMEM(weights.shape, jnp.float32),
                pltpu.VMEM(state.shape, jnp.float32),
                pltpu.VMEM((slots, tables, dim, samples), jnp.bfloat16),
                pltpu.VMEM((slots, tables, dim, samples), jnp.bfloat16),
                pltpu.VMEM((shares, block, samples), jnp.int32),
                pltpu.VMEM((2, chips, shares, block, samples), jnp.int32),
                pltpu.VMEM((3, slots, rows // LOW * dim, LOW), jnp.float32),
                pltpu.VMEM((2, slots, rows // LOW * dim, LOW), jnp.float32),
                pltpu.VMEM(squares, jnp.float32),
                pltpu.VMEM(squares, jnp.float32),
                pltpu.VMEM((chips,) + squares, jnp.float32),
                dma((6,)),
                dma((slots, tables)), dma((slots, tables)),
                dma((shares,)), dma((shares,)),
                dma((chips,)), dma((chips,)),
                dma((2,)), dma((2,)),
                dma((chips,)), dma((chips,)),
                dma((2, slots)), dma((2, slots)),
            ],
            compiler_params=pltpu.CompilerParams(
                collective_id=0, has_side_effects=True, vmem_limit_bytes=60 * 1024 * 1024
            ),
            cost_estimate=pl.CostEstimate(
                flops=4 * slots * tables * samples * rows * dim, bytes_accessed=4 * 1024 * 1024, transcendentals=0
            ),
        )(feature_order, pooled_grad, row_ids, lengths, weights, state)

    return jax.shard_map(
        body,
        mesh=mesh,
        in_specs=(
            P(None, "col", "table"),
            P(None, None, "table"),
            P(None, "table"),
            P(),
            P("table", "col", None),
            P("table", None),
        ),
        out_specs=(P("table", "col", None), P("table", None)),
        check_vma=False,
    )
```

```python
import functools

import jax
import jax.numpy as jnp
from jax import lax
from jax.experimental import pallas as pl
from jax.experimental.pallas import tpu as pltpu
from jax.sharding import PartitionSpec as P

MESH = pl.DeviceIdType.MESH
LOW = 128
DEEP = 12
REACH = 4
STEP = 2


def kernel(
    tables, cols, place_count, order_hbm, grad_hbm, ids_hbm, len_hbm, w_hbm, state_hbm,
    new_w_ref, new_state_ref,
    order_ref, grad_ref, ids_ref, len_ref, w_ref, state_ref,
    send_grad, recv_grad, send_ids, all_ids, acc, partial, own_square, pair_square, squares,
    in_sem, gs_sem, gr_sem, is_sem, ir_sem, cs_sem, cr_sem, ks_sem, kr_sem, qs_sem, qr_sem, ps_sem, pr_sem,
):
    t = lax.axis_index("table")
    c = lax.axis_index("col")
    slots, dim, rows = w_ref.shape
    samples = grad_ref.shape[2]
    highs = rows // LOW
    deep = DEEP
    across = tables // deep
    shares = tables // cols
    chips = cols // 2
    far_blocks = 9 * across
    z, x = t // across, t % across
    y, core = c // 2, c % 2
    mate = (t, y * 2 + (1 - core))

    def wrap(value, size):
        return jnp.where(value >= size, value - size, jnp.where(value < 0, value + size, value))

    def route(block):
        q, dx = block // across, block % across
        ahead = jnp.where(q == 0, dx % 2 == 0, q % 2 == 1)
        far = q <= 8
        reach = jnp.where(q == 0, 4, jnp.where(far, (8 - q) // 2, (12 - q) // 2))
        source = jnp.where(ahead, reach, -reach)
        owner = jnp.where(far, jnp.where(ahead, -STEP, STEP), 0)
        role = jnp.where(far, jnp.where(ahead, 1, 2), 0)
        return source, dx, owner, role

    def send_to(block):
        source, dx, owner, _ = route(block)
        home = wrap(x - dx, across)
        at = wrap(z - source, deep)
        return at * across + home, wrap(at + owner, deep) * across + home

    def chip_peer(step):
        return wrap(y + step, chips)

    loads = [
        pltpu.make_async_copy(src, dst, in_sem.at[n])
        for n, (src, dst) in enumerate((
            (order_hbm, order_ref), (grad_hbm, grad_ref), (len_hbm, len_ref),
            (ids_hbm, ids_ref), (w_hbm, w_ref), (state_hbm, state_ref),
        ))
    ]
    for load in loads:
        load.start()

    barrier = pltpu.get_barrier_semaphore()

    @pl.loop(0, 2 * REACH)
    def _(step):
        away = REACH - step // 2
        plane = wrap(z + jnp.where(step % 2 == 0, away, -away), deep) * across
        for dx in range(across):
            pl.semaphore_signal(barrier, inc=1, device_id=(plane + wrap(x + dx, across), c), device_id_type=MESH)

    @pl.loop(1, chips)
    def _(step):
        pl.semaphore_signal(barrier, inc=1, device_id=(t, chip_peer(step) * 2 + core), device_id_type=MESH)

    for dx in range(1, across):
        pl.semaphore_signal(barrier, inc=1, device_id=(z * across + wrap(x + dx, across), c), device_id_type=MESH)
    pl.semaphore_signal(barrier, inc=1, device_id=mate, device_id_type=MESH)

    loads[0].wait()
    loads[1].wait()

    @pl.loop(0, tables)
    def _(block):
        target, owner = send_to(block)

        @pl.when(target == t)
        def _():
            for slot in range(slots):
                recv_grad[slot, block] = grad_ref[order_ref[slots * owner + slot]]

        @pl.when(target != t)
        def _():
            for slot in range(slots):
                send_grad[slot, block] = grad_ref[order_ref[slots * owner + slot]]

    loads[2].wait()
    loads[3].wait()
    place = lax.broadcasted_iota(jnp.int32, (place_count, samples), 0)
    for share in range(shares):
        _, owner = send_to(c + cols * share)
        live = []
        for slot in range(slots):
            feature = order_ref[slots * owner + slot]
            length = len_ref[pl.ds(feature, 1), :]
            live.append(jnp.where(place < length, ids_ref[feature], -1))
        send_ids[share] = jnp.concatenate(live, axis=0)
    acc[...] = jnp.zeros_like(acc)

    pl.semaphore_wait(barrier, (2 * REACH + 1) * across - 1 + chips - 1 + 1)

    def ids_copy(share):
        return pltpu.make_async_remote_copy(
            src_ref=send_ids.at[share],
            dst_ref=all_ids.at[core, y, share],
            send_sem=is_sem.at[share],
            recv_sem=ir_sem.at[share],
            device_id=(send_to(c + cols * share)[0], c),
            device_id_type=MESH,
        )

    def own_share(share):
        return send_to(c + cols * share)[0] == t

    for share in range(shares):
        @pl.when(own_share(share))
        def _():
            all_ids[core, y, share] = send_ids[share]

        @pl.when(jnp.logical_not(own_share(share)))
        def _():
            ids_copy(share).start()

    def grad_copy(slot, block, target):
        return pltpu.make_async_remote_copy(
            src_ref=send_grad.at[slot, block],
            dst_ref=recv_grad.at[slot, block],
            send_sem=gs_sem.at[slot, block],
            recv_sem=gr_sem.at[slot, block],
            device_id=(target, c),
            device_id_type=MESH,
        )

    def send_blocks(slot, first, last):
        @pl.loop(first, last)
        def _(block):
            target, _ = send_to(block)

            @pl.when(target != t)
            def _():
                grad_copy(slot, block, target).start()

    for slot in range(slots):
        send_blocks(slot, 0, far_blocks)
    for slot in range(slots):
        send_blocks(slot, far_blocks, tables)

    for share in range(shares):
        @pl.when(jnp.logical_not(own_share(share)))
        def _():
            ids_copy(share).wait_recv()

    def chip_ids(peer, owner):
        return pltpu.make_async_remote_copy(
            src_ref=all_ids.at[core, owner],
            dst_ref=all_ids.at[core, owner],
            send_sem=cs_sem.at[peer],
            recv_sem=cr_sem.at[owner],
            device_id=(t, peer * 2 + core),
            device_id_type=MESH,
        )

    @pl.loop(1, chips)
    def _(step):
        chip_ids(chip_peer(step), y).start()

    @pl.loop(1, chips)
    def _(step):
        peer = chip_peer(step)
        chip_ids(peer, peer).wait_recv()

    def mate_ids(owner):
        return pltpu.make_async_remote_copy(
            src_ref=all_ids.at[owner],
            dst_ref=all_ids.at[owner],
            send_sem=ks_sem.at[0],
            recv_sem=kr_sem.at[0],
            device_id=mate,
            device_id_type=MESH,
        )

    mate_ids(core).start()
    mate_ids(1 - core).wait_recv()

    low_line = lax.broadcasted_iota(jnp.int32, (LOW, samples), 0).astype(jnp.float32).astype(jnp.bfloat16)
    one, none = jnp.bfloat16(1.0), jnp.bfloat16(0.0)

    def work(slot, blocks):
        left, right = [], []
        for block in blocks:
            holder = block % cols
            ids = all_ids[holder % 2, holder // 2, block // cols]
            high = (ids >> (LOW.bit_length() - 1)).astype(jnp.float32).astype(jnp.bfloat16)
            low = (ids & (LOW - 1)).astype(jnp.float32).astype(jnp.bfloat16)
            grad = recv_grad[slot, block]
            for p in range(place_count):
                row = slot * place_count + p
                low_row = jnp.broadcast_to(low[row:row + 1], (LOW, samples))
                right.append(jnp.where(low_row == low_line, one, none))
                high_row = jnp.broadcast_to(high[row:row + 1], (dim, samples))
                left.append(jnp.concatenate(
                    [jnp.where(high_row == jnp.bfloat16(h), grad, none) for h in range(highs)], axis=0))
        role = route(blocks[0])[3]
        acc[role, slot] += lax.dot_general(
            jnp.concatenate(left, axis=1), jnp.concatenate(right, axis=1),
            (((1,), (1,)), ((), ())), preferred_element_type=jnp.float32)

    groups = [(0, 2), (1, 3)] if across == 4 else [(dx,) for dx in range(across)]

    def work_blocks(slot, first, last):
        @pl.loop(first // across, last // across)
        def _(q):
            for group in groups:
                blocks = [q * across + dx for dx in group]
                for block in blocks:
                    target, _ = send_to(block)

                    @pl.when(target != t)
                    def _():
                        grad_copy(slot, block, target).wait_recv()
                work(slot, blocks)

    def partial_copy(slot, side):
        return pltpu.make_async_remote_copy(
            src_ref=acc.at[1 + side, slot],
            dst_ref=partial.at[side, slot],
            send_sem=ps_sem.at[side, slot],
            recv_sem=pr_sem.at[side, slot],
            device_id=(wrap(z + (STEP if side else -STEP), deep) * across + x, c),
            device_id_type=MESH,
        )

    for slot in range(slots):
        work_blocks(slot, 0, far_blocks)
        for side in range(2):
            partial_copy(slot, side).start()
    for slot in range(slots):
        work_blocks(slot, far_blocks, tables)

    loads[4].wait()
    loads[5].wait()
    sums = []
    for slot in range(slots):
        for side in range(2):
            partial_copy(slot, side).wait_recv()
        for h in range(highs):
            part = slice(h * dim, (h + 1) * dim)
            total = acc[0, slot, part, :] + partial[0, slot, part, :] + partial[1, slot, part, :]
            acc[0, slot, part, :] = total
            sums.append(jnp.sum(total * total, axis=0, keepdims=True))
    own_square[...] = jnp.concatenate(sums, axis=0)

    mate_square = pltpu.make_async_remote_copy(
        src_ref=own_square,
        dst_ref=pair_square,
        send_sem=ks_sem.at[1],
        recv_sem=kr_sem.at[1],
        device_id=mate,
        device_id_type=MESH,
    )
    mate_square.start()
    mate_square.wait_recv()
    squares[y] = own_square[...] + pair_square[...]

    def square_copy(peer, owner):
        return pltpu.make_async_remote_copy(
            src_ref=squares.at[owner],
            dst_ref=squares.at[owner],
            send_sem=qs_sem.at[peer],
            recv_sem=qr_sem.at[owner],
            device_id=(t, peer * 2 + core),
            device_id_type=MESH,
        )

    for step in range(1, chips):
        square_copy(chip_peer(step), y).start()

    for step in range(1, chips):
        peer = chip_peer(step)
        square_copy(peer, peer).wait_recv()

    total = squares[0]
    for peer in range(1, chips):
        total = total + squares[peer]
    full = dim * cols
    for slot in range(slots):
        for h in range(highs):
            row = slot * highs + h
            span = slice(h * LOW, (h + 1) * LOW)
            new_state = state_ref[slot:slot + 1, span] + total[row:row + 1] / full
            new_state_ref[slot:slot + 1, span] = new_state
            scale = 0.3 / jnp.sqrt(new_state)
            new_w_ref[slot, :, span] = w_ref[slot, :, span] - acc[0, slot, h * dim:(h + 1) * dim, :] * scale

    for share in range(shares):
        @pl.when(jnp.logical_not(own_share(share)))
        def _():
            ids_copy(share).wait_send()

    mate_ids(core).wait_send()
    mate_square.wait_send()

    @pl.loop(1, chips)
    def _(step):
        peer = chip_peer(step)
        chip_ids(peer, y).wait_send()
        square_copy(peer, y).wait_send()

    for slot in range(slots):
        for side in range(2):
            partial_copy(slot, side).wait_send()

    @pl.loop(0, tables)
    def _(block):
        target, _ = send_to(block)

        @pl.when(target != t)
        def _():
            for slot in range(slots):
                grad_copy(slot, block, target).wait_send()


def solution(mesh):
    tables, cols = mesh.shape["table"], mesh.shape["col"]

    def body(pooled_grad, row_ids, lengths, feature_order, weights, state):
        features, width, samples = pooled_grad.shape
        place_count = row_ids.shape[1]
        slots, dim, rows = weights.shape
        shares = tables // cols
        vmem = pl.BlockSpec(memory_space=pltpu.VMEM)
        dma = pltpu.SemaphoreType.DMA
        chips = cols // 2
        block = slots * place_count
        squares = (slots * (rows // LOW), LOW)
        return pl.pallas_call(
            functools.partial(kernel, tables, cols, place_count),
            out_shape=(
                jax.ShapeDtypeStruct(weights.shape, jnp.float32),
                jax.ShapeDtypeStruct(state.shape, jnp.float32),
            ),
            in_specs=[pl.BlockSpec(memory_space=pltpu.HBM)] * 6,
            out_specs=(vmem, vmem),
            scratch_shapes=[
                pltpu.SMEM(feature_order.shape, jnp.int32),
                pltpu.VMEM(pooled_grad.shape, jnp.bfloat16),
                pltpu.VMEM(row_ids.shape, jnp.int32),
                pltpu.VMEM(lengths.shape, jnp.int32),
                pltpu.VMEM(weights.shape, jnp.float32),
                pltpu.VMEM(state.shape, jnp.float32),
                pltpu.VMEM((slots, tables, dim, samples), jnp.bfloat16),
                pltpu.VMEM((slots, tables, dim, samples), jnp.bfloat16),
                pltpu.VMEM((shares, block, samples), jnp.int32),
                pltpu.VMEM((2, chips, shares, block, samples), jnp.int32),
                pltpu.VMEM((3, slots, rows // LOW * dim, LOW), jnp.float32),
                pltpu.VMEM((2, slots, rows // LOW * dim, LOW), jnp.float32),
                pltpu.VMEM(squares, jnp.float32),
                pltpu.VMEM(squares, jnp.float32),
                pltpu.VMEM((chips,) + squares, jnp.float32),
                dma((6,)),
                dma((slots, tables)), dma((slots, tables)),
                dma((shares,)), dma((shares,)),
                dma((chips,)), dma((chips,)),
                dma((2,)), dma((2,)),
                dma((chips,)), dma((chips,)),
                dma((2, slots)), dma((2, slots)),
            ],
            compiler_params=pltpu.CompilerParams(
                collective_id=0, has_side_effects=True, vmem_limit_bytes=60 * 1024 * 1024
            ),
            cost_estimate=pl.CostEstimate(
                flops=4 * slots * tables * samples * rows * dim, bytes_accessed=4 * 1024 * 1024, transcendentals=0
            ),
        )(feature_order, pooled_grad, row_ids, lengths, weights, state)

    return jax.shard_map(
        body,
        mesh=mesh,
        in_specs=(
            P(None, "col", "table"),
            P(None, None, "table"),
            P(None, "table"),
            P(),
            P("table", "col", None),
            P("table", None),
        ),
        out_specs=(P("table", "col", None), P("table", None)),
        check_vma=False,
    )
```

```python
import functools

import jax
import jax.numpy as jnp
from jax import lax
from jax.experimental import pallas as pl
from jax.experimental.pallas import tpu as pltpu
from jax.sharding import PartitionSpec as P

MESH = pl.DeviceIdType.MESH
LOW = 128
DEEP = 12
REACH = 4
STEP = 2


def kernel(
    tables, cols, place_count, order_hbm, grad_hbm, ids_hbm, len_hbm, w_hbm, state_hbm,
    new_w_ref, new_state_ref,
    order_ref, grad_ref, ids_ref, len_ref, w_ref, state_ref,
    send_grad, recv_grad, send_ids, all_ids, acc, partial, own_square, pair_square, squares,
    in_sem, gs_sem, gr_sem, is_sem, ir_sem, cs_sem, cr_sem, ks_sem, kr_sem, qs_sem, qr_sem, ps_sem, pr_sem,
):
    t = lax.axis_index("table")
    c = lax.axis_index("col")
    slots, dim, rows = w_ref.shape
    samples = grad_ref.shape[2]
    highs = rows // LOW
    deep = DEEP
    across = tables // deep
    shares = tables // cols
    chips = cols // 2
    far_blocks = 9 * across
    z, x = t // across, t % across
    y, core = c // 2, c % 2
    mate = (t, y * 2 + (1 - core))

    def wrap(value, size):
        return jnp.where(value >= size, value - size, jnp.where(value < 0, value + size, value))

    def route(block):
        q, dx = block // across, block % across
        ahead = jnp.where(q == 0, dx % 2 == 0, q % 2 == 1)
        far = q <= 8
        reach = jnp.where(q == 0, 4, jnp.where(far, (8 - q) // 2, (12 - q) // 2))
        source = jnp.where(ahead, reach, -reach)
        owner = jnp.where(far, jnp.where(ahead, -STEP, STEP), 0)
        role = jnp.where(far, jnp.where(ahead, 1, 2), 0)
        return source, dx, owner, role

    def send_to(block):
        source, dx, owner, _ = route(block)
        home = wrap(x - dx, across)
        at = wrap(z - source, deep)
        return at * across + home, wrap(at + owner, deep) * across + home

    def chip_peer(step):
        return wrap(y + step, chips)

    loads = [
        pltpu.make_async_copy(src, dst, in_sem.at[n])
        for n, (src, dst) in enumerate((
            (order_hbm, order_ref), (grad_hbm, grad_ref), (len_hbm, len_ref),
            (ids_hbm, ids_ref), (w_hbm, w_ref), (state_hbm, state_ref),
        ))
    ]
    for load in loads:
        load.start()

    barrier = pltpu.get_barrier_semaphore()

    @pl.loop(0, 2 * REACH)
    def _(step):
        away = REACH - step // 2
        plane = wrap(z + jnp.where(step % 2 == 0, away, -away), deep) * across
        for dx in range(across):
            pl.semaphore_signal(barrier, inc=1, device_id=(plane + wrap(x + dx, across), c), device_id_type=MESH)

    @pl.loop(1, chips)
    def _(step):
        pl.semaphore_signal(barrier, inc=1, device_id=(t, chip_peer(step) * 2 + core), device_id_type=MESH)

    for dx in range(1, across):
        pl.semaphore_signal(barrier, inc=1, device_id=(z * across + wrap(x + dx, across), c), device_id_type=MESH)
    pl.semaphore_signal(barrier, inc=1, device_id=mate, device_id_type=MESH)

    loads[0].wait()
    loads[1].wait()

    @pl.loop(0, tables)
    def _(block):
        target, owner = send_to(block)

        @pl.when(target == t)
        def _():
            for slot in range(slots):
                recv_grad[slot, block] = grad_ref[order_ref[slots * owner + slot]]

        @pl.when(target != t)
        def _():
            for slot in range(slots):
                send_grad[slot, block] = grad_ref[order_ref[slots * owner + slot]]

    loads[2].wait()
    loads[3].wait()
    place = lax.broadcasted_iota(jnp.int32, (place_count, samples), 0)
    for share in range(shares):
        _, owner = send_to(c + cols * share)
        live = []
        for slot in range(slots):
            feature = order_ref[slots * owner + slot]
            length = len_ref[pl.ds(feature, 1), :]
            live.append(jnp.where(place < length, ids_ref[feature], -1))
        send_ids[share] = jnp.concatenate(live, axis=0)
    acc[...] = jnp.zeros_like(acc)

    pl.semaphore_wait(barrier, (2 * REACH + 1) * across - 1 + chips - 1 + 1)

    def ids_copy(share):
        return pltpu.make_async_remote_copy(
            src_ref=send_ids.at[share],
            dst_ref=all_ids.at[core, y, share],
            send_sem=is_sem.at[share],
            recv_sem=ir_sem.at[share],
            device_id=(send_to(c + cols * share)[0], c),
            device_id_type=MESH,
        )

    def own_share(share):
        return send_to(c + cols * share)[0] == t

    for share in range(shares):
        @pl.when(own_share(share))
        def _():
            all_ids[core, y, share] = send_ids[share]

        @pl.when(jnp.logical_not(own_share(share)))
        def _():
            ids_copy(share).start()

    def grad_copy(slot, block, target):
        return pltpu.make_async_remote_copy(
            src_ref=send_grad.at[slot, block],
            dst_ref=recv_grad.at[slot, block],
            send_sem=gs_sem.at[slot, block],
            recv_sem=gr_sem.at[slot, block],
            device_id=(target, c),
            device_id_type=MESH,
        )

    def send_blocks(slot, first, last):
        @pl.loop(first, last)
        def _(block):
            target, _ = send_to(block)

            @pl.when(target != t)
            def _():
                grad_copy(slot, block, target).start()

    for slot in range(slots):
        send_blocks(slot, 0, far_blocks)
    for slot in range(slots):
        send_blocks(slot, far_blocks, tables)

    for share in range(shares):
        @pl.when(jnp.logical_not(own_share(share)))
        def _():
            ids_copy(share).wait_recv()

    def chip_ids(peer, owner):
        return pltpu.make_async_remote_copy(
            src_ref=all_ids.at[core, owner],
            dst_ref=all_ids.at[core, owner],
            send_sem=cs_sem.at[peer],
            recv_sem=cr_sem.at[owner],
            device_id=(t, peer * 2 + core),
            device_id_type=MESH,
        )

    @pl.loop(1, chips)
    def _(step):
        chip_ids(chip_peer(step), y).start()

    @pl.loop(1, chips)
    def _(step):
        peer = chip_peer(step)
        chip_ids(peer, peer).wait_recv()

    def mate_ids(owner):
        return pltpu.make_async_remote_copy(
            src_ref=all_ids.at[owner],
            dst_ref=all_ids.at[owner],
            send_sem=ks_sem.at[0],
            recv_sem=kr_sem.at[0],
            device_id=mate,
            device_id_type=MESH,
        )

    mate_ids(core).start()
    mate_ids(1 - core).wait_recv()

    low_line = lax.broadcasted_iota(jnp.int32, (LOW, samples), 0).astype(jnp.float32).astype(jnp.bfloat16)
    one, none = jnp.bfloat16(1.0), jnp.bfloat16(0.0)

    def work(slot, blocks):
        left, right = [], []
        for block in blocks:
            holder = block % cols
            ids = all_ids[holder % 2, holder // 2, block // cols]
            high = (ids >> (LOW.bit_length() - 1)).astype(jnp.float32).astype(jnp.bfloat16)
            low = (ids & (LOW - 1)).astype(jnp.float32).astype(jnp.bfloat16)
            grad = recv_grad[slot, block]
            for p in range(place_count):
                row = slot * place_count + p
                low_row = jnp.broadcast_to(low[row:row + 1], (LOW, samples))
                right.append(jnp.where(low_row == low_line, one, none))
                high_row = jnp.broadcast_to(high[row:row + 1], (dim, samples))
                left.append(jnp.concatenate(
                    [jnp.where(high_row == jnp.bfloat16(h), grad, none) for h in range(highs)], axis=0))
        role = route(blocks[0])[3]
        acc[role, slot] += lax.dot_general(
            jnp.concatenate(left, axis=1), jnp.concatenate(right, axis=1),
            (((1,), (1,)), ((), ())), preferred_element_type=jnp.float32)

    groups = [(0, 2), (1, 3)] if across == 4 else [(dx,) for dx in range(across)]

    def work_blocks(slot, first, last):
        @pl.loop(first // across, last // across)
        def _(q):
            for group in groups:
                blocks = [q * across + dx for dx in group]
                for block in blocks:
                    target, _ = send_to(block)

                    @pl.when(target != t)
                    def _():
                        grad_copy(slot, block, target).wait_recv()
                work(slot, blocks)

    def partial_copy(slot, side):
        return pltpu.make_async_remote_copy(
            src_ref=acc.at[1 + side, slot],
            dst_ref=partial.at[side, slot],
            send_sem=ps_sem.at[side, slot],
            recv_sem=pr_sem.at[side, slot],
            device_id=(wrap(z + (STEP if side else -STEP), deep) * across + x, c),
            device_id_type=MESH,
        )

    for slot in range(slots):
        work_blocks(slot, 0, far_blocks)
        for side in range(2):
            partial_copy(slot, side).start()
    for slot in range(slots):
        work_blocks(slot, far_blocks, tables)

    loads[4].wait()
    loads[5].wait()
    sums = []
    for slot in range(slots):
        for side in range(2):
            partial_copy(slot, side).wait_recv()
        for h in range(highs):
            part = slice(h * dim, (h + 1) * dim)
            total = acc[0, slot, part, :] + partial[0, slot, part, :] + partial[1, slot, part, :]
            acc[0, slot, part, :] = total
            sums.append(jnp.sum(total * total, axis=0, keepdims=True))
    own_square[...] = jnp.concatenate(sums, axis=0)

    mate_square = pltpu.make_async_remote_copy(
        src_ref=own_square,
        dst_ref=pair_square,
        send_sem=ks_sem.at[1],
        recv_sem=kr_sem.at[1],
        device_id=mate,
        device_id_type=MESH,
    )
    mate_square.start()
    mate_square.wait_recv()
    squares[y] = own_square[...] + pair_square[...]

    def square_copy(peer, owner):
        return pltpu.make_async_remote_copy(
            src_ref=squares.at[owner],
            dst_ref=squares.at[owner],
            send_sem=qs_sem.at[peer],
            recv_sem=qr_sem.at[owner],
            device_id=(t, peer * 2 + core),
            device_id_type=MESH,
        )

    for step in sorted(range(1, chips), key=lambda step: -min(step, chips - step)):
        square_copy(chip_peer(step), y).start()

    for step in range(1, chips):
        peer = chip_peer(step)
        square_copy(peer, peer).wait_recv()

    total = squares[0]
    for peer in range(1, chips):
        total = total + squares[peer]
    full = dim * cols
    for slot in range(slots):
        for h in range(highs):
            row = slot * highs + h
            span = slice(h * LOW, (h + 1) * LOW)
            new_state = state_ref[slot:slot + 1, span] + total[row:row + 1] / full
            new_state_ref[slot:slot + 1, span] = new_state
            scale = 0.3 / jnp.sqrt(new_state)
            new_w_ref[slot, :, span] = w_ref[slot, :, span] - acc[0, slot, h * dim:(h + 1) * dim, :] * scale

    for share in range(shares):
        @pl.when(jnp.logical_not(own_share(share)))
        def _():
            ids_copy(share).wait_send()

    mate_ids(core).wait_send()
    mate_square.wait_send()

    @pl.loop(1, chips)
    def _(step):
        peer = chip_peer(step)
        chip_ids(peer, y).wait_send()
        square_copy(peer, y).wait_send()

    for slot in range(slots):
        for side in range(2):
            partial_copy(slot, side).wait_send()

    @pl.loop(0, tables)
    def _(block):
        target, _ = send_to(block)

        @pl.when(target != t)
        def _():
            for slot in range(slots):
                grad_copy(slot, block, target).wait_send()


def solution(mesh):
    tables, cols = mesh.shape["table"], mesh.shape["col"]

    def body(pooled_grad, row_ids, lengths, feature_order, weights, state):
        features, width, samples = pooled_grad.shape
        place_count = row_ids.shape[1]
        slots, dim, rows = weights.shape
        shares = tables // cols
        vmem = pl.BlockSpec(memory_space=pltpu.VMEM)
        dma = pltpu.SemaphoreType.DMA
        chips = cols // 2
        block = slots * place_count
        squares = (slots * (rows // LOW), LOW)
        return pl.pallas_call(
            functools.partial(kernel, tables, cols, place_count),
            out_shape=(
                jax.ShapeDtypeStruct(weights.shape, jnp.float32),
                jax.ShapeDtypeStruct(state.shape, jnp.float32),
            ),
            in_specs=[pl.BlockSpec(memory_space=pltpu.HBM)] * 6,
            out_specs=(vmem, vmem),
            scratch_shapes=[
                pltpu.SMEM(feature_order.shape, jnp.int32),
                pltpu.VMEM(pooled_grad.shape, jnp.bfloat16),
                pltpu.VMEM(row_ids.shape, jnp.int32),
                pltpu.VMEM(lengths.shape, jnp.int32),
                pltpu.VMEM(weights.shape, jnp.float32),
                pltpu.VMEM(state.shape, jnp.float32),
                pltpu.VMEM((slots, tables, dim, samples), jnp.bfloat16),
                pltpu.VMEM((slots, tables, dim, samples), jnp.bfloat16),
                pltpu.VMEM((shares, block, samples), jnp.int32),
                pltpu.VMEM((2, chips, shares, block, samples), jnp.int32),
                pltpu.VMEM((3, slots, rows // LOW * dim, LOW), jnp.float32),
                pltpu.VMEM((2, slots, rows // LOW * dim, LOW), jnp.float32),
                pltpu.VMEM(squares, jnp.float32),
                pltpu.VMEM(squares, jnp.float32),
                pltpu.VMEM((chips,) + squares, jnp.float32),
                dma((6,)),
                dma((slots, tables)), dma((slots, tables)),
                dma((shares,)), dma((shares,)),
                dma((chips,)), dma((chips,)),
                dma((2,)), dma((2,)),
                dma((chips,)), dma((chips,)),
                dma((2, slots)), dma((2, slots)),
            ],
            compiler_params=pltpu.CompilerParams(
                collective_id=0, has_side_effects=True, vmem_limit_bytes=60 * 1024 * 1024
            ),
            cost_estimate=pl.CostEstimate(
                flops=4 * slots * tables * samples * rows * dim, bytes_accessed=4 * 1024 * 1024, transcendentals=0
            ),
        )(feature_order, pooled_grad, row_ids, lengths, weights, state)

    return jax.shard_map(
        body,
        mesh=mesh,
        in_specs=(
            P(None, "col", "table"),
            P(None, None, "table"),
            P(None, "table"),
            P(),
            P("table", "col", None),
            P("table", None),
        ),
        out_specs=(P("table", "col", None), P("table", None)),
        check_vma=False,
    )
```
